128 devices in a mesh: section: 16 (over z_hi, x, core), sp: 8 (over y, z_lo).
Axes of the slice: x: 4, y: 4, z: 4 (z_hi: 2, z_lo: 2; z = z_hi * 2 + z_lo), core: 2. Of those that a mesh axis runs over, the one named last changes fastest.
Arguments:
- section_input: bfloat16 [6144, 3072], P('section'), may hold values from -4 to 4
- patch_of_section: int32 [16], P('section'), may hold values from 0 to 15, each once
- shift_scale: float32 [16, 2, 3072], P('section'), may hold values from -3 to 3
- gate: float32 [16, 3072], P('section'), may hold values from 2 to 6
- w_qkv: bfloat16 [16, 3072, 3, 3072], P('section', None, None, 'sp'), may hold values from -0.109375 to 0.109375
- w_out: bfloat16 [16, 3072, 3072], P('section', 'sp'), may hold values from -0.109375 to 0.109375
- stale_kv: bfloat16 [2, 16, 6144, 3072], P(None, 'section', None, 'sp'), may hold values from -200 to 200
Outputs:
- next_input: bfloat16 [6144, 3072], P('section')
The draws below stay inside these ranges and needn't reach their ends.
Inputs may be any that keep to these rules, and one draw needn't show every extreme that they name: `patch_of_section`: every section works on a different patch.
All inputs are finite; a program needn't handle non-finite values.
Results may differ from the reference program's by a relative error of at most 0.012.
The reference program's roundings to bfloat16 on the way count: a program that leaves them out, or rounds other values in their place, can miss the bound.
Values may be sent and summed in bfloat16 or wider, within the bound.
No kernel may reach another device: no remote copies, remote signals or barrier semaphores. Data moves between devices by JAX's collectives and lax.ppermute only.
A program may use at most 192 MiB of HBM per device.

```python
import jax
import jax.numpy as jnp
from jax import lax

D = 3072
HEADS = 24
HD = 128
PATCH = 384
TOKENS = 6144
ROWS = 6144
N_SECTION = 16


def draw_stale_kv(key, part):
    key = jax.random.fold_in(key, 7)
    noise_key = jax.random.fold_in(key, 0)
    width = HEADS * HD
    entries = jax.random.normal(noise_key, (2, N_SECTION, TOKENS, width), jnp.float32)
    return entries.astype(jnp.bfloat16)


def level_of(key, dims, cuts, smallest, largest):
    def one(axis_at, blocks):
        steps = jax.random.uniform(jax.random.fold_in(jax.random.fold_in(key, 6), axis_at), (blocks,), jnp.float32, smallest / len(cuts), largest / len(cuts))
        return jnp.repeat(jnp.exp(steps), dims[axis_at] // blocks).reshape((-1,) + (1,) * (len(dims) - axis_at - 1))

    gain = one(*cuts[0])
    for cut in cuts[1:]:
        gain = gain * one(*cut)
    return gain


def noise(own_key, extent, deviation, most, pieces=(), dtype=jnp.bfloat16):
    array = jax.random.normal(own_key, extent, jnp.float32) * deviation
    if len(pieces) > 0:
        array = level_of(own_key, extent, pieces, -0.22, 0.18) * array
    return jnp.clip(array, min=-most, max=most).astype(dtype)


def setup_inputs(seed: int = 0) -> dict:
    arg_keys = jax.random.split(jax.random.key(seed), 8)
    return {
        "section_input": noise(arg_keys[0], (ROWS, D), 0.3, 4.0, ((0, 16),)),
        "patch_of_section": jax.random.permutation(arg_keys[1], N_SECTION).astype(jnp.int32),
        "shift_scale": noise(arg_keys[2], (N_SECTION, 2, D), 0.5, 3.0, ((0, 16),), jnp.float32),
        "gate": jnp.clip(2.0 + 4.0 * jax.random.uniform(arg_keys[3], (N_SECTION, D), jnp.float32) ** level_of(arg_keys[3], (N_SECTION, D), ((0, 16),), -0.2, 0.2), 2.0, 6.0),
        "w_qkv": noise(arg_keys[4], (N_SECTION, D, 3, HEADS * HD), D ** -0.5, 0.109375, ((0, 16), (3, 8))),
        "w_out": noise(arg_keys[5], (N_SECTION, HEADS * HD, D), (HEADS * HD) ** -0.5, 0.109375, ((0, 16), (1, 8))),
        "stale_kv": draw_stale_kv(jax.random.fold_in(arg_keys[7], 71), 0),
    }


EPSILON = 1e-06

def modulate(activations, shift_scale):
    floats = activations.astype(jnp.float32)
    centre = lax.optimization_barrier(jnp.mean(floats, axis=-1, keepdims=True))
    spread = lax.optimization_barrier(jnp.mean(jnp.square(floats - centre), axis=-1, keepdims=True))
    normed = (floats - centre) / jnp.sqrt(spread + EPSILON)
    modded = ((1.0 + shift_scale[1]) * normed + shift_scale[0]).astype(jnp.bfloat16)
    return (modded, floats)

def one_head(operands):
    queries, key_rows, value_rows = operands
    scores = jnp.dot(queries, key_rows.T, preferred_element_type=jnp.float32) * HD ** (-0.5)
    maxima = lax.optimization_barrier(jnp.max(scores, axis=-1, keepdims=True))
    expos = jnp.exp(scores - maxima)
    attn_weights = (expos / lax.optimization_barrier(jnp.sum(expos, axis=-1, keepdims=True))).astype(jnp.bfloat16)
    return jnp.dot(attn_weights, value_rows, preferred_element_type=jnp.float32).astype(jnp.bfloat16)

def split_heads(matrix):
    return matrix.reshape(matrix.shape[0], HEADS, HD).transpose(1, 0, 2)

def run_section(operands):
    activations, patch, shift_scale, gate_row, weight_qkv, weight_out, cache = operands
    modded, floats = modulate(activations, shift_scale)
    width = HEADS * HD
    projected = jnp.dot(modded, weight_qkv.reshape(D, 3 * width), preferred_element_type=jnp.float32).astype(jnp.bfloat16)
    queries = projected[:, :width]
    fresh_keys = projected[:, width:2 * width]
    fresh_values = projected[:, 2 * width:]
    start = (patch * PATCH).astype(jnp.int32)
    anchor = jnp.zeros((), jnp.int32)
    key_rows = lax.dynamic_update_slice(cache[0], fresh_keys, (start, anchor))
    value_rows = lax.dynamic_update_slice(cache[1], fresh_values, (start, anchor))
    mixed = lax.map(one_head, (split_heads(queries), split_heads(key_rows), split_heads(value_rows)))
    merged = mixed.transpose(1, 0, 2).reshape(PATCH, width)
    branch = jnp.dot(merged, weight_out, preferred_element_type=jnp.float32)
    return (floats + gate_row * branch).astype(jnp.bfloat16)

def reference(section_input, patch_of_section, shift_scale, gate, w_qkv, w_out, stale_kv):
    outputs = lax.map(run_section, (section_input.reshape(N_SECTION, PATCH, D), patch_of_section, shift_scale, gate, w_qkv, w_out, stale_kv.transpose(1, 0, 2, 3)))
    return jnp.roll(outputs, 1, axis=0).reshape(N_SECTION * PATCH, D)
```

```python
import functools
import math

import jax
import jax.numpy as jnp
from jax import lax
from jax.experimental import pallas as pl
from jax.experimental.pallas import tpu as pltpu
from jax.sharding import PartitionSpec as P

HD = 128
EPSILON = 1e-06
KEY_BLOCK = 512
ROW_TILE = 32
BASE2 = math.log2(math.e) / math.sqrt(HD)
TRANSPOSED = (((1,), (1,)), ((), ()))
VMEM_LIMIT = 56 * 2**20


def modulate(x_ref, shift_scale_ref, modded_ref):
    shift = shift_scale_ref[0:1, :]
    scale = 1.0 + shift_scale_ref[1:2, :]
    for row in range(0, x_ref.shape[0], 16):
        floats = x_ref[row : row + 16, :].astype(jnp.float32)
        centred = floats - jnp.mean(floats, axis=-1, keepdims=True)
        spread = jnp.mean(jnp.square(centred), axis=-1, keepdims=True)
        normed = centred / jnp.sqrt(spread + EPSILON)
        modded_ref[row : row + 16, :] = (scale * normed + shift).astype(jnp.bfloat16)


def attend(heads, rows, q_ref, k_ref, v_ref, scores, probs, acc_ref, max_ref, fade_ref, mixed_ref, need_keys, need_values):
    blocks = k_ref.shape[1] // KEY_BLOCK
    units = [(head, block) for head in range(heads) for block in range(blocks)]

    def score(unit):
        head, block = units[unit]
        if block == 0:
            need_keys(head)
        scores[unit % 2][...] = lax.dot_general(
            q_ref[:, head * HD : (head + 1) * HD],
            k_ref[head, block * KEY_BLOCK : (block + 1) * KEY_BLOCK, :],
            TRANSPOSED,
            preferred_element_type=jnp.float32,
        )

    def weigh(unit):
        _, block = units[unit]
        for row in range(0, rows, ROW_TILE):
            tile = slice(row, row + ROW_TILE)
            s = scores[unit % 2][tile, :]
            top = jnp.max(s, axis=-1, keepdims=True) * BASE2
            if block > 0:
                before = max_ref[tile, :1]
                top = jnp.maximum(before, top)
                fade_ref[tile, :] = jnp.broadcast_to(jnp.exp2(before - top), (ROW_TILE, HD))
            max_ref[tile, :] = jnp.broadcast_to(top, (ROW_TILE, HD))
            probs[unit % 2][tile, :] = jnp.exp2(s * BASE2 - top).astype(jnp.bfloat16)

    def mix(unit):
        head, block = units[unit]
        if block == 0:
            need_values(head)
        part = jnp.dot(
            probs[unit % 2][...],
            v_ref[head, block * KEY_BLOCK : (block + 1) * KEY_BLOCK, :],
            preferred_element_type=jnp.float32,
        )
        if block == 0:
            acc_ref[...] = part
        else:
            fade = fade_ref[...]
            acc_ref[:, :HD] = acc_ref[:, :HD] * fade + part[:, :HD]
            acc_ref[:, HD:] = acc_ref[:, HD:] * fade + part[:, HD:]
        if block == blocks - 1:
            mixed_ref[:, head * HD : (head + 1) * HD] = (acc_ref[:, :HD] / acc_ref[:, HD:]).astype(jnp.bfloat16)

    score(0)
    for unit in range(len(units) + 1):
        if unit + 1 < len(units):
            score(unit + 1)
        if unit >= 1:
            mix(unit - 1)
        if unit < len(units):
            weigh(unit)


def section_kernel(
    place_ref, x_ref, shift_scale_ref, w_qkv_ref, w_out_ref, kv_ref, *refs, heads, ring
):
    outs, refs = refs[:ring], refs[ring:]
    (w_buf, out_buf, k_buf, v_buf, modded, q_buf, fresh, score0, score1, prob0, prob1,
     acc_ref, max_ref, fade_ref, mixed_ref, sems) = refs
    patch = place_ref[0]
    ring_index = place_ref[1]
    rows, width = q_buf.shape
    block = rows // ring

    weights = [pltpu.make_async_copy(w_qkv_ref.at[j], w_buf.at[j], sems.at[j]) for j in range(3)]
    keys = [
        pltpu.make_async_copy(kv_ref.at[0, :, pl.ds(h * HD, HD)], k_buf.at[h], sems.at[3 + h])
        for h in range(heads)
    ]
    values = [
        pltpu.make_async_copy(
            kv_ref.at[1, :, pl.ds(h * HD, HD)], v_buf.at[h, :, pl.ds(0, HD)], sems.at[3 + heads + h]
        )
        for h in range(heads)
    ]
    out_weight = pltpu.make_async_copy(w_out_ref, out_buf, sems.at[3 + 2 * heads])
    for copy in weights:
        copy.start()
    modulate(x_ref, shift_scale_ref, modded)
    for head in range(heads):
        keys[head].start()
        values[head].start()
    out_weight.start()
    v_buf[:, :, HD:] = jnp.ones((heads, v_buf.shape[1], HD), jnp.bfloat16)
    for j in range(3):
        weights[j].wait()
        part = jnp.dot(modded[...], w_buf[j], preferred_element_type=jnp.float32).astype(jnp.bfloat16)
        if j == 0:
            for k in range(ring):
                turned = pl.multiple_of(lax.rem(k - ring_index + ring, ring) * block, block)
                q_buf[pl.ds(turned, block), :] = part[k * block : (k + 1) * block, :]
        else:
            fresh[j - 1] = part

    first = pl.multiple_of(patch * rows, rows)

    def need_keys(head):
        keys[head].wait()
        k_buf[head, pl.ds(first, rows), :] = fresh[0, :, head * HD : (head + 1) * HD]

    def need_values(head):
        values[head].wait()
        v_buf[head, pl.ds(first, rows), :HD] = fresh[1, :, head * HD : (head + 1) * HD]

    attend(heads, rows, q_buf, k_buf, v_buf, (score0, score1), (prob0, prob1), acc_ref, max_ref, fade_ref,
           mixed_ref, need_keys, need_values)
    out_weight.wait()
    for column in range(0, out_buf.shape[1], 512):
        part = jnp.dot(mixed_ref[...], out_buf[:, column : column + 512], preferred_element_type=jnp.float32)
        for k in range(ring):
            outs[k][:, column : column + 512] = part[k * block : (k + 1) * block, :].astype(jnp.bfloat16)


def section(place, x, shift_scale, w_qkv, w_out, kv, ring):
    rows, features = x.shape
    tokens, width = kv.shape[1:]
    heads = width // HD
    vmem = pl.BlockSpec(memory_space=pltpu.VMEM)
    hbm = pl.BlockSpec(memory_space=pl.ANY)
    return pl.pallas_call(
        functools.partial(section_kernel, heads=heads, ring=ring),
        out_shape=[jax.ShapeDtypeStruct((rows // ring, features), jnp.bfloat16)] * ring,
        in_specs=[pl.BlockSpec(memory_space=pltpu.SMEM), vmem, vmem, hbm, hbm, hbm],
        out_specs=[vmem] * ring,
        scratch_shapes=[
            pltpu.VMEM((3, features, width), jnp.bfloat16),
            pltpu.VMEM((width, features), jnp.bfloat16),
            pltpu.VMEM((heads, tokens, HD), jnp.bfloat16),
            pltpu.VMEM((heads, tokens, 2 * HD), jnp.bfloat16),
            pltpu.VMEM((rows, features), jnp.bfloat16),
            pltpu.VMEM((rows, width), jnp.bfloat16),
            pltpu.VMEM((2, rows, width), jnp.bfloat16),
            pltpu.VMEM((rows, KEY_BLOCK), jnp.float32),
            pltpu.VMEM((rows, KEY_BLOCK), jnp.float32),
            pltpu.VMEM((rows, KEY_BLOCK), jnp.bfloat16),
            pltpu.VMEM((rows, KEY_BLOCK), jnp.bfloat16),
            pltpu.VMEM((rows, 2 * HD), jnp.float32),
            pltpu.VMEM((rows, HD), jnp.float32),
            pltpu.VMEM((rows, HD), jnp.float32),
            pltpu.VMEM((rows, width), jnp.bfloat16),
            pltpu.SemaphoreType.DMA((4 + 2 * heads,)),
        ],
        compiler_params=pltpu.CompilerParams(vmem_limit_bytes=VMEM_LIMIT),
    )(place, x, shift_scale, w_qkv, w_out, kv)


def assemble_kernel(place_ref, *refs):
    parts, out_ref, sems = refs[:-2], refs[-2], refs[-1]
    ring = len(parts)
    block = parts[0].shape[0]
    copies = []
    for k, part in enumerate(parts):
        row = pl.multiple_of(lax.rem(place_ref[1] - k + ring, ring) * block, block)
        copies.append(pltpu.make_async_copy(part, out_ref.at[pl.ds(row, block), :], sems.at[k]))
    for copy in copies:
        copy.start()
    for copy in copies:
        copy.wait()


def assemble(place, parts):
    block, features = parts[0].shape
    hbm = pl.BlockSpec(memory_space=pl.ANY)
    return pl.pallas_call(
        assemble_kernel,
        out_shape=jax.ShapeDtypeStruct((block * len(parts), features), jnp.bfloat16),
        in_specs=[pl.BlockSpec(memory_space=pltpu.SMEM)] + [hbm] * len(parts),
        out_specs=hbm,
        scratch_shapes=[pltpu.SemaphoreType.DMA((len(parts),))],
    )(place, *parts)


def body(section_input, patch_of_section, shift_scale, gate, w_qkv, w_out, stale_kv):
    sections, group = lax.axis_size("section"), lax.axis_size("sp")
    pair = 2
    ring = group // pair

    def moved(array, sections_on, ring_on, pair_on):
        route = []
        for s in range(sections):
            for r in range(ring):
                for p in range(pair):
                    target = ((s + sections_on) % sections * ring + (r + ring_on) % ring) * pair + (p + pair_on) % pair
                    route.append(((s * ring + r) * pair + p, target))
        return lax.ppermute(array, ("section", "sp"), route)

    ring_index = lax.axis_index("sp") // pair
    place = jnp.stack([patch_of_section[0], ring_index.astype(jnp.int32)])
    parts = section(place, section_input, shift_scale[0], jnp.transpose(w_qkv[0], (1, 0, 2)), w_out[0],
                    stale_kv[:, 0], ring)
    total = parts[0].astype(jnp.float32)
    for k in range(1, ring):
        total = total + moved(parts[k], 0, k, 0).astype(jnp.float32)
    mine = total.astype(jnp.bfloat16)
    other = moved(mine, 0, 0, 1)
    block = mine.shape[0]
    own_rows = lax.dynamic_slice_in_dim(section_input, ring_index * block, block, 0).astype(jnp.float32)
    branch = mine.astype(jnp.float32) + other.astype(jnp.float32)
    updated = (own_rows + gate[0] * branch).astype(jnp.bfloat16)
    return assemble(place, [moved(updated, 1, k, 0) for k in range(ring)])


def solution(mesh):
    in_specs = (
        P("section", None),
        P("section"),
        P("section", None, None),
        P("section", None),
        P("section", None, None, "sp"),
        P("section", "sp", None),
        P(None, "section", None, "sp"),
    )
    out_specs = P("section", None)
    return jax.shard_map(body, mesh=mesh, in_specs=in_specs, out_specs=out_specs, check_vma=False)
```

```python
import functools
import math

import jax
import jax.numpy as jnp
from jax import lax
from jax.experimental import pallas as pl
from jax.experimental.pallas import tpu as pltpu
from jax.sharding import PartitionSpec as P

HD = 128
EPSILON = 1e-06
KEY_BLOCK = 512
ROW_TILE = 32
BASE2 = math.log2(math.e) / math.sqrt(HD)
TRANSPOSED = (((1,), (1,)), ((), ()))
VMEM_LIMIT = 56 * 2**20


def modulate(x_ref, shift_scale_ref, modded_ref):
    shift = shift_scale_ref[0:1, :]
    scale = 1.0 + shift_scale_ref[1:2, :]
    for row in range(0, x_ref.shape[0], 16):
        floats = x_ref[row : row + 16, :].astype(jnp.float32)
        centred = floats - jnp.mean(floats, axis=-1, keepdims=True)
        spread = jnp.mean(jnp.square(centred), axis=-1, keepdims=True)
        normed = centred / jnp.sqrt(spread + EPSILON)
        modded_ref[row : row + 16, :] = (scale * normed + shift).astype(jnp.bfloat16)


def attend(heads, rows, q_ref, k_ref, v_ref, scores, probs, acc_ref, max_ref, fade_ref, mixed_ref, need_keys, need_values):
    blocks = k_ref.shape[1] // KEY_BLOCK
    units = [(head, block) for head in range(heads) for block in range(blocks)]

    def score(unit):
        head, block = units[unit]
        if block == 0:
            need_keys(head)
        scores[unit % 2][...] = lax.dot_general(
            q_ref[:, head * HD : (head + 1) * HD],
            k_ref[head, block * KEY_BLOCK : (block + 1) * KEY_BLOCK, :],
            TRANSPOSED,
            preferred_element_type=jnp.float32,
        )

    def weigh(unit):
        _, block = units[unit]
        for row in range(0, rows, ROW_TILE):
            tile = slice(row, row + ROW_TILE)
            s = scores[unit % 2][tile, :]
            top = jnp.max(s, axis=-1, keepdims=True) * BASE2
            if block > 0:
                before = max_ref[tile, :1]
                top = jnp.maximum(before, top)
                fade_ref[tile, :] = jnp.broadcast_to(jnp.exp2(before - top), (ROW_TILE, HD))
            max_ref[tile, :] = jnp.broadcast_to(top, (ROW_TILE, HD))
            probs[unit % 2][tile, :] = jnp.exp2(s * BASE2 - top).astype(jnp.bfloat16)

    def mix(unit):
        head, block = units[unit]
        if block == 0:
            need_values(head)
        part = jnp.dot(
            probs[unit % 2][...],
            v_ref[head, block * KEY_BLOCK : (block + 1) * KEY_BLOCK, :],
            preferred_element_type=jnp.float32,
        )
        if block == 0:
            acc_ref[...] = part
        else:
            fade = fade_ref[...]
            acc_ref[:, :HD] = acc_ref[:, :HD] * fade + part[:, :HD]
            acc_ref[:, HD:] = acc_ref[:, HD:] * fade + part[:, HD:]
        if block == blocks - 1:
            mixed_ref[:, head * HD : (head + 1) * HD] = (acc_ref[:, :HD] / acc_ref[:, HD:]).astype(jnp.bfloat16)

    score(0)
    for unit in range(len(units) + 1):
        if unit + 1 < len(units):
            score(unit + 1)
        if unit >= 1:
            mix(unit - 1)
        if unit < len(units):
            weigh(unit)


def section_kernel(patch_ref, x_ref, shift_scale_ref, w_qkv_ref, w_out_ref, kv_ref, *refs, ring, pair):
    straight, refs = refs[:ring], refs[ring:]
    (kept, crossed, w_buf, out_buf, k_buf, v_buf, modded, q_buf, fresh, score0, score1, prob0, prob1,
     acc_ref, max_ref, fade_ref, mixed_ref, sems) = refs
    heads = k_buf.shape[0]
    rows = q_buf.shape[0]
    share = rows // (ring * pair)
    half = out_buf.shape[1] // 2
    place = lax.axis_index("sp")
    ring_index, pair_index = place // pair, lax.rem(place, pair)

    weights = [pltpu.make_async_copy(w_qkv_ref.at[j], w_buf.at[j], sems.at[j]) for j in range(3)]
    keys = [
        pltpu.make_async_copy(kv_ref.at[0, :, pl.ds(h * HD, HD)], k_buf.at[h], sems.at[3 + h])
        for h in range(heads)
    ]
    values = [
        pltpu.make_async_copy(
            kv_ref.at[1, :, pl.ds(h * HD, HD)], v_buf.at[h, :, pl.ds(0, HD)], sems.at[3 + heads + h]
        )
        for h in range(heads)
    ]
    out_weight = pltpu.make_async_copy(w_out_ref, out_buf, sems.at[3 + 2 * heads])
    for copy in weights:
        copy.start()
    modulate(x_ref, shift_scale_ref, modded)
    for head in range(heads):
        keys[head].start()
        values[head].start()
    out_weight.start()
    v_buf[:, :, HD:] = jnp.ones((heads, v_buf.shape[1], HD), jnp.bfloat16)
    for j in range(3):
        weights[j].wait()
        part = jnp.dot(modded[...], w_buf[j], preferred_element_type=jnp.float32).astype(jnp.bfloat16)
        if j > 0:
            fresh[j - 1] = part
            continue
        for r in range(ring):
            for p in range(pair):
                steps = lax.rem(r - ring_index + ring, ring)
                turned = pl.multiple_of((steps * pair + lax.rem(p + pair_index, pair)) * share, share)
                row = (r * pair + p) * share
                q_buf[pl.ds(turned, share), :] = part[row : row + share, :]

    first = pl.multiple_of(patch_ref[0] * rows, rows)

    def need_keys(head):
        keys[head].wait()
        k_buf[head, pl.ds(first, rows), :] = fresh[0, :, head * HD : (head + 1) * HD]

    def need_values(head):
        values[head].wait()
        v_buf[head, pl.ds(first, rows), :HD] = fresh[1, :, head * HD : (head + 1) * HD]

    attend(heads, rows, q_buf, k_buf, v_buf, (score0, score1), (prob0, prob1), acc_ref, max_ref, fade_ref,
           mixed_ref, need_keys, need_values)
    out_weight.wait()
    for column in range(0, 2 * half, 512):
        part = jnp.dot(mixed_ref[...], out_buf[:, column : column + 512], preferred_element_type=jnp.float32)
        part = part.astype(jnp.bfloat16)
        for k in range(ring):
            row = k * pair * share
            if column < half:
                straight[k][:, column : column + 512] = part[row : row + pair * share, :]
            else:
                place = slice(column - half, column - half + 512)
                kept[k * share : (k + 1) * share, place] = part[row : row + share, :]
                crossed[k * share : (k + 1) * share, place] = part[row + share : row + 2 * share, :]


def section(patch, x, shift_scale, w_qkv, w_out, kv, ring, pair):
    rows, features = x.shape
    tokens, width = kv.shape[1:]
    heads = width // HD
    smem = pl.BlockSpec(memory_space=pltpu.SMEM)
    vmem = pl.BlockSpec(memory_space=pltpu.VMEM)
    hbm = pl.BlockSpec(memory_space=pl.ANY)
    results = pl.pallas_call(
        functools.partial(section_kernel, ring=ring, pair=pair),
        out_shape=[jax.ShapeDtypeStruct((rows // ring, features // 2), jnp.bfloat16)] * ring
        + [jax.ShapeDtypeStruct((rows // pair, features // 2), jnp.bfloat16)] * 2,
        in_specs=[smem, vmem, vmem, hbm, hbm, hbm],
        out_specs=[vmem] * (ring + 2),
        scratch_shapes=[
            pltpu.VMEM((3, features, width), jnp.bfloat16),
            pltpu.VMEM((width, features), jnp.bfloat16),
            pltpu.VMEM((heads, tokens, HD), jnp.bfloat16),
            pltpu.VMEM((heads, tokens, 2 * HD), jnp.bfloat16),
            pltpu.VMEM((rows, features), jnp.bfloat16),
            pltpu.VMEM((rows, width), jnp.bfloat16),
            pltpu.VMEM((2, rows, width), jnp.bfloat16),
            pltpu.VMEM((rows, KEY_BLOCK), jnp.float32),
            pltpu.VMEM((rows, KEY_BLOCK), jnp.float32),
            pltpu.VMEM((rows, KEY_BLOCK), jnp.bfloat16),
            pltpu.VMEM((rows, KEY_BLOCK), jnp.bfloat16),
            pltpu.VMEM((rows, 2 * HD), jnp.float32),
            pltpu.VMEM((rows, HD), jnp.float32),
            pltpu.VMEM((rows, HD), jnp.float32),
            pltpu.VMEM((rows, width), jnp.bfloat16),
            pltpu.SemaphoreType.DMA((4 + 2 * heads,)),
        ],
        compiler_params=pltpu.CompilerParams(vmem_limit_bytes=VMEM_LIMIT),
    )(patch, x, shift_scale, w_qkv, w_out, kv)
    return results[:ring], results[ring], results[ring + 1]


def assemble_kernel(*refs, ring, pair):
    left, (kept, crossed, out_ref, sems) = refs[:ring], refs[ring:]
    place = lax.axis_index("sp")
    ring_index, pair_index = place // pair, lax.rem(place, pair)
    share = kept.shape[0] // ring
    half = kept.shape[1]
    copies = []
    for k in range(ring):
        for c in range(pair):
            source = lax.rem(ring_index - k + ring, ring) * pair + lax.rem(pair_index + c, pair)
            rows = pl.ds(pl.multiple_of(source * share, share), share)
            right = (kept, crossed)[c]
            for side, piece in enumerate((left[k].at[pl.ds(c * share, share)], right.at[pl.ds(k * share, share)])):
                target = out_ref.at[rows, pl.ds(side * half, half)]
                copies.append(pltpu.make_async_copy(piece, target, sems.at[len(copies)]))
    for copy in copies:
        copy.start()
    for copy in copies:
        copy.wait()


def assemble(left, kept, crossed, pair):
    ring = len(left)
    rows, half = kept.shape
    return pl.pallas_call(
        functools.partial(assemble_kernel, ring=ring, pair=pair),
        out_shape=jax.ShapeDtypeStruct((rows * pair, 2 * half), kept.dtype),
        in_specs=[pl.BlockSpec(memory_space=pl.ANY)] * (ring + 2),
        out_specs=pl.BlockSpec(memory_space=pltpu.VMEM),
        scratch_shapes=[pltpu.SemaphoreType.DMA((2 * ring * pair,))],
    )(*left, kept, crossed)


def body(section_input, patch_of_section, shift_scale, gate, w_qkv, w_out, stale_kv):
    sections, group = lax.axis_size("section"), lax.axis_size("sp")
    pair = 2
    ring = group // pair

    def moved(array, sections_on, ring_on, pair_on):
        route = []
        for s in range(sections):
            for r in range(ring):
                for p in range(pair):
                    target = ((s + sections_on) % sections * ring + (r + ring_on) % ring) * pair + (p + pair_on) % pair
                    route.append(((s * ring + r) * pair + p, target))
        return lax.ppermute(array, ("section", "sp"), route)

    def wide(array):
        return array.astype(jnp.float32)

    def narrow(array):
        return array.astype(jnp.bfloat16)

    share = section_input.shape[0] // group
    half = section_input.shape[1] // 2
    around = range(1, ring)
    straight, kept, crossed = section(
        patch_of_section, section_input, shift_scale[0], jnp.transpose(w_qkv[0], (1, 0, 2)), w_out[0],
        stale_kv[:, 0], ring, pair,
    )
    crossed = moved(crossed, 0, 0, 1)
    straight = [straight[0]] + [moved(straight[k], 0, k, 0) for k in around]
    left = sum(wide(piece) for piece in straight)
    right = wide(kept) + wide(crossed)
    left = left[:share] + wide(moved(narrow(left[share:]), 0, 0, 1))
    right = [right[k * share : (k + 1) * share] for k in range(ring)]
    right = right[0] + sum(wide(moved(narrow(right[k]), 0, k, 0)) for k in around)
    own = wide(lax.dynamic_slice_in_dim(section_input, lax.axis_index("sp") * share, share, 0))
    left = narrow(own[:, :half] + gate[0, :half] * left)
    right = narrow(own[:, half:] + gate[0, half:] * right)
    left = jnp.concatenate([moved(left, 1, 0, 0), moved(left, 1, 0, 1)])
    right = jnp.concatenate([moved(right, 1, k, 0) for k in range(ring)])
    crossed = moved(right, 0, 0, 1)
    return assemble([left] + [moved(left, 0, k, 0) for k in around], right, crossed, pair)


def solution(mesh):
    in_specs = (
        P("section", None),
        P("section"),
        P("section", None, None),
        P("section", None),
        P("section", None, None, "sp"),
        P("section", "sp", None),
        P(None, "section", None, "sp"),
    )
    out_specs = P("section", None)
    return jax.shard_map(body, mesh=mesh, in_specs=in_specs, out_specs=out_specs, check_vma=False)
```

```python
import functools
import math

import jax
import jax.numpy as jnp
from jax import lax
from jax.experimental import pallas as pl
from jax.experimental.pallas import tpu as pltpu
from jax.sharding import PartitionSpec as P

HD = 128
EPSILON = 1e-06
KEY_BLOCK = 512
ROW_TILE = 32
X_PIECES = 4
BASE2 = math.log2(math.e) / math.sqrt(HD)
TRANSPOSED = (((1,), (1,)), ((), ()))
VMEM_LIMIT = 56 * 2**20


def modulate(x_ref, shift_scale_ref, modded_ref, first, last):
    shift = shift_scale_ref[0:1, :]
    scale = 1.0 + shift_scale_ref[1:2, :]
    for row in range(first, last, 16):
        floats = x_ref[row : row + 16, :].astype(jnp.float32)
        centred = floats - jnp.mean(floats, axis=-1, keepdims=True)
        spread = jnp.mean(jnp.square(centred), axis=-1, keepdims=True)
        normed = centred * lax.rsqrt(spread + EPSILON)
        modded_ref[row : row + 16, :] = (scale * normed + shift).astype(jnp.bfloat16)


def attend(heads, rows, q_ref, k_ref, v_ref, scores, probs, acc_ref, max_ref, fade_ref, mixed_ref, need_keys, need_values):
    blocks = k_ref.shape[1] // KEY_BLOCK
    units = [(head, block) for head in range(heads) for block in range(blocks)]

    def score(unit):
        head, block = units[unit]
        if block == 0:
            need_keys(head)
        scores[unit % 2][...] = lax.dot_general(
            q_ref[:, head * HD : (head + 1) * HD],
            k_ref[head, block * KEY_BLOCK : (block + 1) * KEY_BLOCK, :],
            TRANSPOSED,
            preferred_element_type=jnp.float32,
        )

    def weigh(unit):
        _, block = units[unit]
        for row in range(0, rows, ROW_TILE):
            tile = slice(row, row + ROW_TILE)
            s = scores[unit % 2][tile, :]
            top = jnp.max(s, axis=-1, keepdims=True) * BASE2
            if block > 0:
                before = max_ref[tile, :1]
                top = jnp.maximum(before, top)
                fade_ref[tile, :] = jnp.broadcast_to(jnp.exp2(before - top), (ROW_TILE, HD))
            max_ref[tile, :] = jnp.broadcast_to(top, (ROW_TILE, HD))
            probs[unit % 2][tile, :] = jnp.exp2(s * BASE2 - top).astype(jnp.bfloat16)

    def mix(unit):
        head, block = units[unit]
        if block == 0:
            need_values(head)
        part = jnp.dot(
            probs[unit % 2][...],
            v_ref[head, block * KEY_BLOCK : (block + 1) * KEY_BLOCK, :],
            preferred_element_type=jnp.float32,
        )
        if block == 0:
            acc_ref[...] = part
        else:
            fade = fade_ref[...]
            acc_ref[:, :HD] = acc_ref[:, :HD] * fade + part[:, :HD]
            acc_ref[:, HD:] = acc_ref[:, HD:] * fade + part[:, HD:]
        if block == blocks - 1:
            mixed_ref[:, head * HD : (head + 1) * HD] = (acc_ref[:, :HD] / acc_ref[:, HD:]).astype(jnp.bfloat16)

    score(0)
    for unit in range(len(units) + 1):
        if unit + 1 < len(units):
            score(unit + 1)
        if unit >= 1:
            mix(unit - 1)
        if unit < len(units):
            weigh(unit)


def section_kernel(patch_hbm, shift_scale_hbm, x_ref, w_qkv_ref, w_out_ref, kv_ref, *refs, ring, pair):
    straight, refs = refs[:ring], refs[ring:]
    (kept, crossed, x_buf, w_buf, out_buf, k_buf, v_buf, modded, q_buf, fresh, score0, score1, prob0, prob1,
     acc_ref, max_ref, fade_ref, mixed_ref, patch_ref, shift_scale_ref, sems, x_sems, out_sems) = refs
    heads = k_buf.shape[0]
    rows, features = x_buf.shape
    share = rows // (ring * pair)
    half = features // 2
    place = lax.axis_index("sp")
    ring_index, pair_index = place // pair, lax.rem(place, pair)

    piece = rows // X_PIECES
    inputs = [
        pltpu.make_async_copy(x_ref.at[pl.ds(i * piece, piece)], x_buf.at[pl.ds(i * piece, piece)], x_sems.at[i])
        for i in range(X_PIECES)
    ]
    weights = [pltpu.make_async_copy(w_qkv_ref.at[j], w_buf.at[j], sems.at[j]) for j in range(3)]
    keys = [
        pltpu.make_async_copy(kv_ref.at[0, :, pl.ds(h * HD, HD)], k_buf.at[h], sems.at[3 + h])
        for h in range(heads)
    ]
    values = [
        pltpu.make_async_copy(
            kv_ref.at[1, :, pl.ds(h * HD, HD)], v_buf.at[h, :, pl.ds(0, HD)], sems.at[3 + heads + h]
        )
        for h in range(heads)
    ]
    out_weight = pltpu.make_async_copy(w_out_ref, out_buf, sems.at[3 + 2 * heads])
    small = [
        pltpu.make_async_copy(shift_scale_hbm, shift_scale_ref, x_sems.at[X_PIECES]),
        pltpu.make_async_copy(patch_hbm, patch_ref, x_sems.at[X_PIECES + 1]),
    ]
    for copy in (*inputs, *small, weights[0]):
        copy.start()
    for copy in small:
        copy.wait()
    for i in range(X_PIECES):
        inputs[i].wait()
        if i == 0:
            weights[1].start()
            weights[2].start()
        modulate(x_buf, shift_scale_ref, modded, i * piece, (i + 1) * piece)
    keys[0].start()
    values[0].start()
    v_buf[:, :, HD:] = jnp.ones((heads, v_buf.shape[1], HD), jnp.bfloat16)
    for j in range(3):
        weights[j].wait()
        if j == 1:
            for head in range(1, heads):
                keys[head].start()
                values[head].start()
            out_weight.start()
        part = jnp.dot(modded[...], w_buf[j], preferred_element_type=jnp.float32).astype(jnp.bfloat16)
        if j > 0:
            fresh[j - 1] = part
            continue
        for r in range(ring):
            for p in range(pair):
                steps = lax.rem(r - ring_index + ring, ring)
                turned = pl.multiple_of((steps * pair + lax.rem(p + pair_index, pair)) * share, share)
                row = (r * pair + p) * share
                q_buf[pl.ds(turned, share), :] = part[row : row + share, :]

    first = pl.multiple_of(patch_ref[0] * rows, rows)

    def need_keys(head):
        keys[head].wait()
        k_buf[head, pl.ds(first, rows), :] = fresh[0, :, head * HD : (head + 1) * HD]

    def need_values(head):
        values[head].wait()
        v_buf[head, pl.ds(first, rows), :HD] = fresh[1, :, head * HD : (head + 1) * HD]

    attend(heads, rows, q_buf, k_buf, v_buf, (score0, score1), (prob0, prob1), acc_ref, max_ref, fade_ref,
           mixed_ref, need_keys, need_values)
    out_weight.wait()
    results = []

    def leave(row, count, column, width, target):
        copy = pltpu.make_async_copy(x_buf.at[pl.ds(row, count), pl.ds(column, width)], target, out_sems.at[len(results)])
        copy.start()
        results.append(copy)

    for column in [*range(half, features, 512), *range(0, half, 512)]:
        part = jnp.dot(mixed_ref[...], out_buf[:, column : column + 512], preferred_element_type=jnp.float32)
        x_buf[:, column : column + 512] = part.astype(jnp.bfloat16)
        for k in range(ring):
            row = k * pair * share
            if column < half:
                leave(row, pair * share, column, 512, straight[k].at[:, pl.ds(column, 512)])
            else:
                for c, target in enumerate((kept, crossed)):
                    leave(row + c * share, share, column, 512,
                          target.at[pl.ds(k * share, share), pl.ds(column - half, 512)])
    for copy in results:
        copy.wait()


def section(patch, x, shift_scale, w_qkv, w_out, kv, ring, pair):
    rows, features = x.shape
    tokens, width = kv.shape[1:]
    heads = width // HD
    hbm = pl.BlockSpec(memory_space=pl.ANY)
    results = pl.pallas_call(
        functools.partial(section_kernel, ring=ring, pair=pair),
        out_shape=[jax.ShapeDtypeStruct((rows // ring, features // 2), jnp.bfloat16)] * ring
        + [jax.ShapeDtypeStruct((rows // pair, features // 2), jnp.bfloat16)] * 2,
        in_specs=[hbm] * 6,
        out_specs=[hbm] * (ring + 2),
        scratch_shapes=[
            pltpu.VMEM((rows, features), jnp.bfloat16),
            pltpu.VMEM((3, features, width), jnp.bfloat16),
            pltpu.VMEM((width, features), jnp.bfloat16),
            pltpu.VMEM((heads, tokens, HD), jnp.bfloat16),
            pltpu.VMEM((heads, tokens, 2 * HD), jnp.bfloat16),
            pltpu.VMEM((rows, features), jnp.bfloat16),
            pltpu.VMEM((rows, width), jnp.bfloat16),
            pltpu.VMEM((2, rows, width), jnp.bfloat16),
            pltpu.VMEM((rows, KEY_BLOCK), jnp.float32),
            pltpu.VMEM((rows, KEY_BLOCK), jnp.float32),
            pltpu.VMEM((rows, KEY_BLOCK), jnp.bfloat16),
            pltpu.VMEM((rows, KEY_BLOCK), jnp.bfloat16),
            pltpu.VMEM((rows, 2 * HD), jnp.float32),
            pltpu.VMEM((rows, HD), jnp.float32),
            pltpu.VMEM((rows, HD), jnp.float32),
            pltpu.VMEM((rows, width), jnp.bfloat16),
            pltpu.SMEM((1,), jnp.int32),
            pltpu.VMEM((2, features), jnp.float32),
            pltpu.SemaphoreType.DMA((4 + 2 * heads,)),
            pltpu.SemaphoreType.DMA((X_PIECES + 2,)),
            pltpu.SemaphoreType.DMA((features // 2 // 512 * ring * (1 + pair),)),
        ],
        compiler_params=pltpu.CompilerParams(vmem_limit_bytes=VMEM_LIMIT),
    )(patch, shift_scale, x, w_qkv, w_out, kv)
    return results[:ring], results[ring], results[ring + 1]


def assemble_kernel(*refs, ring, pair):
    kept, crossed, *left, out_ref, sems = refs
    place = lax.axis_index("sp")
    ring_index, pair_index = place // pair, lax.rem(place, pair)
    share = kept.shape[0] // ring
    half = kept.shape[1]
    copies = []
    for k in range(ring):
        for c in range(pair):
            source = lax.rem(ring_index - k + ring, ring) * pair + lax.rem(pair_index + c, pair)
            rows = pl.ds(pl.multiple_of(source * share, share), share)
            right = (kept, crossed)[c]
            for side, piece in enumerate((left[k].at[pl.ds(c * share, share)], right.at[pl.ds(k * share, share)])):
                target = out_ref.at[rows, pl.ds(side * half, half)]
                copies.append(pltpu.make_async_copy(piece, target, sems.at[len(copies)]))
    for copy in copies:
        copy.start()
    for copy in copies:
        copy.wait()


def assemble(left, kept, crossed, pair):
    ring = len(left)
    rows, half = kept.shape
    return pl.pallas_call(
        functools.partial(assemble_kernel, ring=ring, pair=pair),
        out_shape=jax.ShapeDtypeStruct((rows * pair, 2 * half), kept.dtype),
        in_specs=[pl.BlockSpec(memory_space=pl.ANY)] * (ring + 2),
        out_specs=pl.BlockSpec(memory_space=pl.ANY),
        scratch_shapes=[pltpu.SemaphoreType.DMA((2 * ring * pair,))],
        compiler_params=pltpu.CompilerParams(vmem_limit_bytes=2**20),
    )(kept, crossed, *left)


def body(section_input, patch_of_section, shift_scale, gate, w_qkv, w_out, stale_kv):
    sections, group = lax.axis_size("section"), lax.axis_size("sp")
    pair = 2
    ring = group // pair

    def moved(array, sections_on, ring_on, pair_on):
        route = []
        for s in range(sections):
            for r in range(ring):
                for p in range(pair):
                    target = ((s + sections_on) % sections * ring + (r + ring_on) % ring) * pair + (p + pair_on) % pair
                    route.append(((s * ring + r) * pair + p, target))
        return lax.ppermute(array, ("section", "sp"), route)

    def wide(array):
        return array.astype(jnp.float32)

    def narrow(array):
        return array.astype(jnp.bfloat16)

    share = section_input.shape[0] // group
    half = section_input.shape[1] // 2
    around = range(1, ring)
    straight, kept, crossed = section(
        patch_of_section, section_input, shift_scale[0], jnp.transpose(w_qkv[0], (1, 0, 2)), w_out[0],
        stale_kv[:, 0], ring, pair,
    )
    crossed = moved(crossed, 0, 0, 1)
    straight = [straight[0]] + [moved(straight[k], 0, k, 0) for k in around]
    right = wide(kept) + wide(crossed)
    left = sum(wide(piece) for piece in straight)
    own = wide(lax.dynamic_slice_in_dim(section_input, lax.axis_index("sp") * share, share, 0))
    left_gate, right_gate = gate[0, :half], gate[0, half:]
    right_own = moved(narrow(own[:, half:] + right_gate * right[:share]), 1, 0, 0)
    right_parts = [moved(narrow(right_gate * right[k * share : (k + 1) * share]), 1, k, 0) for k in around]
    left_own = moved(narrow(own[:, :half] + left_gate * left[:share]), 1, 0, 0)
    left_part = moved(narrow(left_gate * left[share:]), 1, 0, 1)
    right = narrow(wide(right_own) + sum(wide(part) for part in right_parts))
    left = narrow(wide(left_own) + wide(left_part))
    right = jnp.concatenate([right] + [moved(right, 0, k, 0) for k in around])
    left = jnp.concatenate([left, moved(left, 0, 0, 1)])
    return assemble([left] + [moved(left, 0, k, 0) for k in around], right, moved(right, 0, 0, 1), pair)


def solution(mesh):
    in_specs = (
        P("section", None),
        P("section"),
        P("section", None, None),
        P("section", None),
        P("section", None, None, "sp"),
        P("section", "sp", None),
        P(None, "section", None, "sp"),
    )
    out_specs = P("section", None)
    return jax.shard_map(body, mesh=mesh, in_specs=in_specs, out_specs=out_specs, check_vma=False)
```

```python
import functools
import math

import jax
import jax.numpy as jnp
from jax import lax
from jax.experimental import pallas as pl
from jax.experimental.pallas import tpu as pltpu
from jax.sharding import PartitionSpec as P

HD = 128
EPSILON = 1e-06
KEY_BLOCK = 512
ROW_TILE = 32
X_PIECES = 4
BASE2 = math.log2(math.e) / math.sqrt(HD)
TRANSPOSED = (((1,), (1,)), ((), ()))
VMEM_LIMIT = 56 * 2**20


def modulate(x_ref, shift_scale_ref, modded_ref, first, last):
    shift = shift_scale_ref[0:1, :]
    scale = 1.0 + shift_scale_ref[1:2, :]
    for row in range(first, last, 16):
        floats = x_ref[row : row + 16, :].astype(jnp.float32)
        centred = floats - jnp.mean(floats, axis=-1, keepdims=True)
        spread = jnp.mean(jnp.square(centred), axis=-1, keepdims=True)
        normed = centred * lax.rsqrt(spread + EPSILON)
        modded_ref[row : row + 16, :] = (scale * normed + shift).astype(jnp.bfloat16)


def attend(heads, rows, q_ref, k_ref, v_ref, scores, probs, acc_ref, max_ref, fade_ref, mixed_ref, need_keys, need_values):
    blocks = k_ref.shape[1] // KEY_BLOCK
    units = [(head, block) for head in range(heads) for block in range(blocks)]

    def score(unit):
        head, block = units[unit]
        if block == 0:
            need_keys(head)
        scores[unit % 2][...] = lax.dot_general(
            q_ref[:, head * HD : (head + 1) * HD],
            k_ref[head, block * KEY_BLOCK : (block + 1) * KEY_BLOCK, :],
            TRANSPOSED,
            preferred_element_type=jnp.float32,
        )

    def weigh(unit):
        _, block = units[unit]
        for row in range(0, rows, ROW_TILE):
            tile = slice(row, row + ROW_TILE)
            s = scores[unit % 2][tile, :]
            top = jnp.max(s, axis=-1, keepdims=True) * BASE2
            if block > 0:
                before = max_ref[tile, :1]
                top = jnp.maximum(before, top)
                fade_ref[tile, :] = jnp.broadcast_to(jnp.exp2(before - top), (ROW_TILE, HD))
            max_ref[tile, :] = jnp.broadcast_to(top, (ROW_TILE, HD))
            probs[unit % 2][tile, :] = jnp.exp2(s * BASE2 - top).astype(jnp.bfloat16)

    def mix(unit):
        head, block = units[unit]
        if block == 0:
            need_values(head)
        part = jnp.dot(
            probs[unit % 2][...],
            v_ref[head, block * KEY_BLOCK : (block + 1) * KEY_BLOCK, :],
            preferred_element_type=jnp.float32,
        )
        if block == 0:
            acc_ref[...] = part
        else:
            fade = fade_ref[...]
            acc_ref[:, :HD] = acc_ref[:, :HD] * fade + part[:, :HD]
            acc_ref[:, HD:] = acc_ref[:, HD:] * fade + part[:, HD:]
        if block == blocks - 1:
            mixed_ref[:, head * HD : (head + 1) * HD] = (acc_ref[:, :HD] / acc_ref[:, HD:]).astype(jnp.bfloat16)

    score(0)
    for unit in range(len(units) + 1):
        if unit + 1 < len(units):
            score(unit + 1)
        if unit >= 1:
            mix(unit - 1)
        if unit < len(units):
            weigh(unit)


def section_kernel(patch_hbm, shift_scale_hbm, x_ref, w_qkv_ref, w_out_ref, kv_ref, *refs, ring, pair):
    straight, refs = refs[:ring], refs[ring:]
    (kept, crossed, x_buf, w_buf, out_buf, k_buf, v_buf, modded, q_buf, fresh, score0, score1, prob0, prob1,
     acc_ref, max_ref, fade_ref, mixed_ref, patch_ref, shift_scale_ref, sems, x_sems, out_sems) = refs
    heads = k_buf.shape[0]
    rows, features = x_buf.shape
    share = rows // (ring * pair)
    half = features // 2
    place = lax.axis_index("sp")
    ring_index, pair_index = place // pair, lax.rem(place, pair)

    piece = rows // X_PIECES
    inputs = [
        pltpu.make_async_copy(x_ref.at[pl.ds(i * piece, piece)], x_buf.at[pl.ds(i * piece, piece)], x_sems.at[i])
        for i in range(X_PIECES)
    ]
    weights = [pltpu.make_async_copy(w_qkv_ref.at[j], w_buf.at[j], sems.at[j]) for j in range(3)]
    keys = [
        pltpu.make_async_copy(kv_ref.at[0, :, pl.ds(h * HD, HD)], k_buf.at[h], sems.at[3 + h])
        for h in range(heads)
    ]
    values = [
        pltpu.make_async_copy(
            kv_ref.at[1, :, pl.ds(h * HD, HD)], v_buf.at[h, :, pl.ds(0, HD)], sems.at[3 + heads + h]
        )
        for h in range(heads)
    ]
    out_weight = pltpu.make_async_copy(w_out_ref, out_buf, sems.at[3 + 2 * heads])
    small = [
        pltpu.make_async_copy(shift_scale_hbm, shift_scale_ref, x_sems.at[X_PIECES]),
        pltpu.make_async_copy(patch_hbm, patch_ref, x_sems.at[X_PIECES + 1]),
    ]
    for copy in (*inputs, *small, weights[0]):
        copy.start()
    v_buf[:, :, HD:] = jnp.ones((heads, v_buf.shape[1], HD), jnp.bfloat16)
    for copy in small:
        copy.wait()
    for i in range(X_PIECES):
        inputs[i].wait()
        if i == 0:
            weights[1].start()
            weights[2].start()
        modulate(x_buf, shift_scale_ref, modded, i * piece, (i + 1) * piece)
    keys[0].start()
    values[0].start()
    for j in range(3):
        weights[j].wait()
        if j == 1:
            for head in range(1, heads):
                keys[head].start()
                values[head].start()
            out_weight.start()
        part = jnp.dot(modded[...], w_buf[j], preferred_element_type=jnp.float32).astype(jnp.bfloat16)
        if j > 0:
            fresh[j - 1] = part
            continue
        for r in range(ring):
            for p in range(pair):
                steps = lax.rem(r - ring_index + ring, ring)
                turned = pl.multiple_of((steps * pair + lax.rem(p + pair_index, pair)) * share, share)
                row = (r * pair + p) * share
                q_buf[pl.ds(turned, share), :] = part[row : row + share, :]

    first = pl.multiple_of(patch_ref[0] * rows, rows)

    def need_keys(head):
        keys[head].wait()
        k_buf[head, pl.ds(first, rows), :] = fresh[0, :, head * HD : (head + 1) * HD]

    def need_values(head):
        values[head].wait()
        v_buf[head, pl.ds(first, rows), :HD] = fresh[1, :, head * HD : (head + 1) * HD]

    attend(heads, rows, q_buf, k_buf, v_buf, (score0, score1), (prob0, prob1), acc_ref, max_ref, fade_ref,
           mixed_ref, need_keys, need_values)
    out_weight.wait()
    results = []

    def leave(row, count, column, width, target):
        copy = pltpu.make_async_copy(x_buf.at[pl.ds(row, count), pl.ds(column, width)], target, out_sems.at[len(results)])
        copy.start()
        results.append(copy)

    for column in [*range(half, features, 512), *range(0, half, 512)]:
        part = jnp.dot(mixed_ref[...], out_buf[:, column : column + 512], preferred_element_type=jnp.float32)
        x_buf[:, column : column + 512] = part.astype(jnp.bfloat16)
        for k in range(ring):
            row = k * pair * share
            if column < half:
                leave(row, pair * share, column, 512, straight[k].at[:, pl.ds(column, 512)])
            else:
                for c, target in enumerate((kept, crossed)):
                    leave(row + c * share, share, column, 512,
                          target.at[pl.ds(k * share, share), pl.ds(column - half, 512)])
    for copy in results:
        copy.wait()


def section(patch, x, shift_scale, w_qkv, w_out, kv, ring, pair):
    rows, features = x.shape
    tokens, width = kv.shape[1:]
    heads = width // HD
    hbm = pl.BlockSpec(memory_space=pl.ANY)
    results = pl.pallas_call(
        functools.partial(section_kernel, ring=ring, pair=pair),
        out_shape=[jax.ShapeDtypeStruct((rows // ring, features // 2), jnp.bfloat16)] * ring
        + [jax.ShapeDtypeStruct((rows // pair, features // 2), jnp.bfloat16)] * 2,
        in_specs=[hbm] * 6,
        out_specs=[hbm] * (ring + 2),
        scratch_shapes=[
            pltpu.VMEM((rows, features), jnp.bfloat16),
            pltpu.VMEM((3, features, width), jnp.bfloat16),
            pltpu.VMEM((width, features), jnp.bfloat16),
            pltpu.VMEM((heads, tokens, HD), jnp.bfloat16),
            pltpu.VMEM((heads, tokens, 2 * HD), jnp.bfloat16),
            pltpu.VMEM((rows, features), jnp.bfloat16),
            pltpu.VMEM((rows, width), jnp.bfloat16),
            pltpu.VMEM((2, rows, width), jnp.bfloat16),
            pltpu.VMEM((rows, KEY_BLOCK), jnp.float32),
            pltpu.VMEM((rows, KEY_BLOCK), jnp.float32),
            pltpu.VMEM((rows, KEY_BLOCK), jnp.bfloat16),
            pltpu.VMEM((rows, KEY_BLOCK), jnp.bfloat16),
            pltpu.VMEM((rows, 2 * HD), jnp.float32),
            pltpu.VMEM((rows, HD), jnp.float32),
            pltpu.VMEM((rows, HD), jnp.float32),
            pltpu.VMEM((rows, width), jnp.bfloat16),
            pltpu.SMEM((1,), jnp.int32),
            pltpu.VMEM((2, features), jnp.float32),
            pltpu.SemaphoreType.DMA((4 + 2 * heads,)),
            pltpu.SemaphoreType.DMA((X_PIECES + 2,)),
            pltpu.SemaphoreType.DMA((features // 2 // 512 * ring * (1 + pair),)),
        ],
        compiler_params=pltpu.CompilerParams(vmem_limit_bytes=VMEM_LIMIT),
    )(patch, shift_scale, x, w_qkv, w_out, kv)
    return results[:ring], results[ring], results[ring + 1]


def assemble_kernel(*refs, ring, pair):
    kept, crossed, *left, out_ref, sems = refs
    place = lax.axis_index("sp")
    ring_index, pair_index = place // pair, lax.rem(place, pair)
    share = kept.shape[0] // ring
    half = kept.shape[1]
    copies = []
    for k in range(ring):
        for c in range(pair):
            source = lax.rem(ring_index - k + ring, ring) * pair + lax.rem(pair_index + c, pair)
            rows = pl.ds(pl.multiple_of(source * share, share), share)
            right = (kept, crossed)[c]
            for side, piece in enumerate((left[k].at[pl.ds(c * share, share)], right.at[pl.ds(k * share, share)])):
                target = out_ref.at[rows, pl.ds(side * half, half)]
                copies.append(pltpu.make_async_copy(piece, target, sems.at[len(copies)]))
    for copy in copies:
        copy.start()
    for copy in copies:
        copy.wait()


def assemble(left, kept, crossed, pair):
    ring = len(left)
    rows, half = kept.shape
    return pl.pallas_call(
        functools.partial(assemble_kernel, ring=ring, pair=pair),
        out_shape=jax.ShapeDtypeStruct((rows * pair, 2 * half), kept.dtype),
        in_specs=[pl.BlockSpec(memory_space=pl.ANY)] * (ring + 2),
        out_specs=pl.BlockSpec(memory_space=pl.ANY),
        scratch_shapes=[pltpu.SemaphoreType.DMA((2 * ring * pair,))],
        compiler_params=pltpu.CompilerParams(vmem_limit_bytes=2**20),
    )(kept, crossed, *left)


def body(section_input, patch_of_section, shift_scale, gate, w_qkv, w_out, stale_kv):
    sections, group = lax.axis_size("section"), lax.axis_size("sp")
    pair = 2
    ring = group // pair

    def moved(array, sections_on, ring_on, pair_on):
        route = []
        for s in range(sections):
            for r in range(ring):
                for p in range(pair):
                    target = ((s + sections_on) % sections * ring + (r + ring_on) % ring) * pair + (p + pair_on) % pair
                    route.append(((s * ring + r) * pair + p, target))
        return lax.ppermute(array, ("section", "sp"), route)

    def wide(array):
        return array.astype(jnp.float32)

    def narrow(array):
        return array.astype(jnp.bfloat16)

    share = section_input.shape[0] // group
    half = section_input.shape[1] // 2
    around = range(1, ring)
    straight, kept, crossed = section(
        patch_of_section, section_input, shift_scale[0], jnp.transpose(w_qkv[0], (1, 0, 2)), w_out[0],
        stale_kv[:, 0], ring, pair,
    )
    crossed = moved(crossed, 0, 0, 1)
    arrived = [moved(straight[k], 0, k, 0) for k in around]
    right = wide(kept) + wide(crossed)
    left = lax.optimization_barrier(wide(straight[0])) + sum(wide(piece) for piece in arrived)
    own = wide(lax.dynamic_slice_in_dim(section_input, lax.axis_index("sp") * share, share, 0))
    left_gate, right_gate = gate[0, :half], gate[0, half:]
    right_own = moved(narrow(own[:, half:] + right_gate * right[:share]), 1, 0, 0)
    right_parts = [moved(narrow(right_gate * right[k * share : (k + 1) * share]), 1, k, 0) for k in around]
    left_own = moved(narrow(own[:, :half] + left_gate * left[:share]), 1, 0, 0)
    left_part = moved(narrow(left_gate * left[share:]), 1, 0, 1)
    right = narrow(wide(right_own) + sum(wide(part) for part in right_parts))
    left = narrow(wide(left_own) + wide(left_part))
    right = jnp.concatenate([right] + [moved(right, 0, k, 0) for k in around])
    left = jnp.concatenate([left, moved(left, 0, 0, 1)])
    return assemble([left] + [moved(left, 0, k, 0) for k in around], right, moved(right, 0, 0, 1), pair)


def solution(mesh):
    in_specs = (
        P("section", None),
        P("section"),
        P("section", None, None),
        P("section", None),
        P("section", None, None, "sp"),
        P("section", "sp", None),
        P(None, "section", None, "sp"),
    )
    out_specs = P("section", None)
    return jax.shard_map(body, mesh=mesh, in_specs=in_specs, out_specs=out_specs, check_vma=False)
```

```python
import functools
import math

import jax
import jax.numpy as jnp
from jax import lax
from jax.experimental import pallas as pl
from jax.experimental.pallas import tpu as pltpu
from jax.sharding import PartitionSpec as P

HD = 128
EPSILON = 1e-06
KEY_BLOCK = 512
ROW_TILE = 32
X_PIECES = 4
BASE2 = math.log2(math.e) / math.sqrt(HD)
TRANSPOSED = (((1,), (1,)), ((), ()))
VMEM_LIMIT = 56 * 2**20


def modulate(x_ref, shift_scale_ref, modded_ref, first, last):
    shift = shift_scale_ref[0:1, :]
    scale = 1.0 + shift_scale_ref[1:2, :]
    for row in range(first, last, 16):
        floats = x_ref[row : row + 16, :].astype(jnp.float32)
        centred = floats - jnp.mean(floats, axis=-1, keepdims=True)
        spread = jnp.mean(jnp.square(centred), axis=-1, keepdims=True)
        normed = centred * lax.rsqrt(spread + EPSILON)
        modded_ref[row : row + 16, :] = (scale * normed + shift).astype(jnp.bfloat16)


def attend(heads, rows, q_ref, k_ref, v_ref, scores, probs, acc_ref, max_ref, fade_ref, mixed_ref, need_keys, need_values):
    blocks = k_ref.shape[1] // KEY_BLOCK
    units = [(head, block) for head in range(heads) for block in range(blocks)]

    def score(unit):
        head, block = units[unit]
        if block == 0:
            need_keys(head)
        scores[unit % 2][...] = lax.dot_general(
            q_ref[:, head * HD : (head + 1) * HD],
            k_ref[head, block * KEY_BLOCK : (block + 1) * KEY_BLOCK, :],
            TRANSPOSED,
            preferred_element_type=jnp.float32,
        )

    def weigh(unit):
        _, block = units[unit]
        for row in range(0, rows, ROW_TILE):
            tile = slice(row, row + ROW_TILE)
            s = scores[unit % 2][tile, :]
            top = jnp.max(s, axis=-1, keepdims=True) * BASE2
            if block > 0:
                before = max_ref[tile, :1]
                top = jnp.maximum(before, top)
                fade_ref[tile, :] = jnp.broadcast_to(jnp.exp2(before - top), (ROW_TILE, HD))
            max_ref[tile, :] = jnp.broadcast_to(top, (ROW_TILE, HD))
            probs[unit % 2][tile, :] = jnp.exp2(s * BASE2 - top).astype(jnp.bfloat16)

    def mix(unit):
        head, block = units[unit]
        if block == 0:
            need_values(head)
        part = jnp.dot(
            probs[unit % 2][...],
            v_ref[head, block * KEY_BLOCK : (block + 1) * KEY_BLOCK, :],
            preferred_element_type=jnp.float32,
        )
        if block == 0:
            acc_ref[...] = part
        else:
            fade = fade_ref[...]
            acc_ref[:, :HD] = acc_ref[:, :HD] * fade + part[:, :HD]
            acc_ref[:, HD:] = acc_ref[:, HD:] * fade + part[:, HD:]
        if block == blocks - 1:
            mixed_ref[:, head * HD : (head + 1) * HD] = (acc_ref[:, :HD] / acc_ref[:, HD:]).astype(jnp.bfloat16)

    score(0)
    for unit in range(len(units) + 1):
        if unit + 1 < len(units):
            score(unit + 1)
        if unit >= 1:
            mix(unit - 1)
        if unit < len(units):
            weigh(unit)


def section_kernel(patch_hbm, shift_scale_hbm, x_ref, w_qkv_ref, w_out_ref, kv_ref, *refs, ring, pair):
    straight, refs = refs[:ring], refs[ring:]
    (kept, crossed, x_buf, w_buf, out_buf, k_buf, v_buf, modded, q_buf, fresh, score0, score1, prob0, prob1,
     acc_ref, max_ref, fade_ref, mixed_ref, patch_ref, shift_scale_ref, sems, x_sems, out_sems) = refs
    heads = k_buf.shape[0]
    rows, features = x_buf.shape
    share = rows // (ring * pair)
    half = features // 2
    place = lax.axis_index("sp")
    ring_index, pair_index = place // pair, lax.rem(place, pair)

    piece = rows // X_PIECES
    inputs = [
        pltpu.make_async_copy(x_ref.at[pl.ds(i * piece, piece)], x_buf.at[pl.ds(i * piece, piece)], x_sems.at[i])
        for i in range(X_PIECES)
    ]
    weights = [pltpu.make_async_copy(w_qkv_ref.at[j], w_buf.at[j], sems.at[j]) for j in range(3)]
    keys = [
        pltpu.make_async_copy(kv_ref.at[0, :, pl.ds(h * HD, HD)], k_buf.at[h], sems.at[3 + h])
        for h in range(heads)
    ]
    values = [
        pltpu.make_async_copy(
            kv_ref.at[1, :, pl.ds(h * HD, HD)], v_buf.at[h, :, pl.ds(0, HD)], sems.at[3 + heads + h]
        )
        for h in range(heads)
    ]
    out_weight = pltpu.make_async_copy(w_out_ref, out_buf, sems.at[3 + 2 * heads])
    small = [
        pltpu.make_async_copy(shift_scale_hbm, shift_scale_ref, x_sems.at[X_PIECES]),
        pltpu.make_async_copy(patch_hbm, patch_ref, x_sems.at[X_PIECES + 1]),
    ]
    for copy in (*inputs, *small, weights[0]):
        copy.start()
    v_buf[:, :, HD:] = jnp.ones((heads, v_buf.shape[1], HD), jnp.bfloat16)
    for copy in small:
        copy.wait()
    for i in range(X_PIECES):
        inputs[i].wait()
        if i == 0:
            weights[1].start()
            weights[2].start()
        modulate(x_buf, shift_scale_ref, modded, i * piece, (i + 1) * piece)
    keys[0].start()
    values[0].start()
    for j in range(3):
        weights[j].wait()
        if j == 1:
            for head in range(1, heads):
                keys[head].start()
                values[head].start()
            out_weight.start()
        part = jnp.dot(modded[...], w_buf[j], preferred_element_type=jnp.float32).astype(jnp.bfloat16)
        if j > 0:
            fresh[j - 1] = part
            continue
        for r in range(ring):
            for p in range(pair):
                steps = lax.rem(r - ring_index + ring, ring)
                turned = pl.multiple_of((steps * pair + lax.rem(p + pair_index, pair)) * share, share)
                row = (r * pair + p) * share
                q_buf[pl.ds(turned, share), :] = part[row : row + share, :]

    first = pl.multiple_of(patch_ref[0] * rows, rows)

    def need_keys(head):
        keys[head].wait()
        k_buf[head, pl.ds(first, rows), :] = fresh[0, :, head * HD : (head + 1) * HD]

    def need_values(head):
        values[head].wait()
        v_buf[head, pl.ds(first, rows), :HD] = fresh[1, :, head * HD : (head + 1) * HD]

    attend(heads, rows, q_buf, k_buf, v_buf, (score0, score1), (prob0, prob1), acc_ref, max_ref, fade_ref,
           mixed_ref, need_keys, need_values)
    out_weight.wait()
    results = []

    def leave(row, count, column, width, target):
        copy = pltpu.make_async_copy(x_buf.at[pl.ds(row, count), pl.ds(column, width)], target, out_sems.at[len(results)])
        copy.start()
        results.append(copy)

    for column in [*range(half, features, 512), *range(0, half, 512)]:
        part = jnp.dot(mixed_ref[...], out_buf[:, column : column + 512], preferred_element_type=jnp.float32)
        x_buf[:, column : column + 512] = part.astype(jnp.bfloat16)
        for k in range(ring):
            row = k * pair * share
            if column < half:
                leave(row, pair * share, column, 512, straight[k].at[:, pl.ds(column, 512)])
            else:
                for c, target in enumerate((kept, crossed)):
                    leave(row + c * share, share, column, 512,
                          target.at[pl.ds(k * share, share), pl.ds(column - half, 512)])
    for copy in results:
        copy.wait()


def section(patch, x, shift_scale, w_qkv, w_out, kv, ring, pair):
    rows, features = x.shape
    tokens, width = kv.shape[1:]
    heads = width // HD
    hbm = pl.BlockSpec(memory_space=pl.ANY)
    results = pl.pallas_call(
        functools.partial(section_kernel, ring=ring, pair=pair),
        out_shape=[jax.ShapeDtypeStruct((rows // ring, features // 2), jnp.bfloat16)] * ring
        + [jax.ShapeDtypeStruct((rows // pair, features // 2), jnp.bfloat16)] * 2,
        in_specs=[hbm] * 6,
        out_specs=[hbm] * (ring + 2),
        scratch_shapes=[
            pltpu.VMEM((rows, features), jnp.bfloat16),
            pltpu.VMEM((3, features, width), jnp.bfloat16),
            pltpu.VMEM((width, features), jnp.bfloat16),
            pltpu.VMEM((heads, tokens, HD), jnp.bfloat16),
            pltpu.VMEM((heads, tokens, 2 * HD), jnp.bfloat16),
            pltpu.VMEM((rows, features), jnp.bfloat16),
            pltpu.VMEM((rows, width), jnp.bfloat16),
            pltpu.VMEM((2, rows, width), jnp.bfloat16),
            pltpu.VMEM((rows, KEY_BLOCK), jnp.float32),
            pltpu.VMEM((rows, KEY_BLOCK), jnp.float32),
            pltpu.VMEM((rows, KEY_BLOCK), jnp.bfloat16),
            pltpu.VMEM((rows, KEY_BLOCK), jnp.bfloat16),
            pltpu.VMEM((rows, 2 * HD), jnp.float32),
            pltpu.VMEM((rows, HD), jnp.float32),
            pltpu.VMEM((rows, HD), jnp.float32),
            pltpu.VMEM((rows, width), jnp.bfloat16),
            pltpu.SMEM((1,), jnp.int32),
            pltpu.VMEM((2, features), jnp.float32),
            pltpu.SemaphoreType.DMA((4 + 2 * heads,)),
            pltpu.SemaphoreType.DMA((X_PIECES + 2,)),
            pltpu.SemaphoreType.DMA((features // 2 // 512 * ring * (1 + pair),)),
        ],
        compiler_params=pltpu.CompilerParams(vmem_limit_bytes=VMEM_LIMIT),
    )(patch, shift_scale, x, w_qkv, w_out, kv)
    return results[:ring], results[ring], results[ring + 1]


def assemble_kernel(*refs, ring, pair):
    kept, crossed, *left, out_ref, sems = refs
    place = lax.axis_index("sp")
    ring_index, pair_index = place // pair, lax.rem(place, pair)
    share = kept.shape[0] // ring
    half = kept.shape[1]
    copies = []
    for k in range(ring):
        for c in range(pair):
            source = lax.rem(ring_index - k + ring, ring) * pair + lax.rem(pair_index + c, pair)
            rows = pl.ds(pl.multiple_of(source * share, share), share)
            right = (kept, crossed)[c]
            for side, piece in enumerate((left[k].at[pl.ds(c * share, share)], right.at[pl.ds(k * share, share)])):
                target = out_ref.at[rows, pl.ds(side * half, half)]
                copies.append(pltpu.make_async_copy(piece, target, sems.at[len(copies)]))
    for copy in copies:
        copy.start()
    for copy in copies:
        copy.wait()


def assemble(left, kept, crossed, pair):
    ring = len(left)
    rows, half = kept.shape
    return pl.pallas_call(
        functools.partial(assemble_kernel, ring=ring, pair=pair),
        out_shape=jax.ShapeDtypeStruct((rows * pair, 2 * half), kept.dtype),
        in_specs=[pl.BlockSpec(memory_space=pl.ANY)] * (ring + 2),
        out_specs=pl.BlockSpec(memory_space=pl.ANY),
        scratch_shapes=[pltpu.SemaphoreType.DMA((2 * ring * pair,))],
        compiler_params=pltpu.CompilerParams(vmem_limit_bytes=2**20),
    )(kept, crossed, *left)


def body(section_input, patch_of_section, shift_scale, gate, w_qkv, w_out, stale_kv):
    sections, group = lax.axis_size("section"), lax.axis_size("sp")
    pair = 2
    ring = group // pair

    def moved(array, sections_on, ring_on, pair_on):
        route = []
        for s in range(sections):
            for r in range(ring):
                for p in range(pair):
                    target = ((s + sections_on) % sections * ring + (r + ring_on) % ring) * pair + (p + pair_on) % pair
                    route.append(((s * ring + r) * pair + p, target))
        return lax.ppermute(array, ("section", "sp"), route)

    def wide(array):
        return array.astype(jnp.float32)

    def narrow(array):
        return array.astype(jnp.bfloat16)

    share = section_input.shape[0] // group
    half = section_input.shape[1] // 2
    around = range(1, ring)
    straight, kept, crossed = section(
        patch_of_section, section_input, shift_scale[0], jnp.transpose(w_qkv[0], (1, 0, 2)), w_out[0],
        stale_kv[:, 0], ring, pair,
    )
    crossed = moved(crossed, 0, 0, 1)
    arrived = [moved(straight[k], 0, k, 0) for k in around]
    right = wide(kept) + wide(crossed)
    left = lax.optimization_barrier(wide(straight[0])) + sum(wide(piece) for piece in arrived)
    own = wide(lax.dynamic_slice_in_dim(section_input, lax.axis_index("sp") * share, share, 0))
    left_gate, right_gate = gate[0, :half], gate[0, half:]
    right_parts = [moved(narrow(right_gate * right[k * share : (k + 1) * share]), 1, k, 0) for k in around]
    own = moved(narrow(own + gate[0] * jnp.concatenate([left[:share], right[:share]], 1)), 1, 0, 0)
    left_part = moved(narrow(left_gate * left[share:]), 1, 0, 1)
    right = narrow(wide(own[:, half:]) + sum(wide(part) for part in right_parts))
    left = narrow(wide(own[:, :half]) + wide(left_part))
    right = jnp.concatenate([right] + [moved(right, 0, k, 0) for k in around])
    left = jnp.concatenate([left, moved(left, 0, 0, 1)])
    return assemble([left] + [moved(left, 0, k, 0) for k in around], right, moved(right, 0, 0, 1), pair)


def solution(mesh):
    in_specs = (
        P("section", None),
        P("section"),
        P("section", None, None),
        P("section", None),
        P("section", None, None, "sp"),
        P("section", "sp", None),
        P(None, "section", None, "sp"),
    )
    out_specs = P("section", None)
    return jax.shard_map(body, mesh=mesh, in_specs=in_specs, out_specs=out_specs, check_vma=False)
```
